1024 devices in a mesh: blk: 32 (over x_lo, z), shard: 32 (over y, x_hi, core).
Axes of the slice: x: 4 (x_hi: 2, x_lo: 2; x = x_hi * 2 + x_lo), y: 8, z: 16, core: 2. Of those that a mesh axis runs over, the one named last changes fastest.
Arguments:
- features: bfloat16 [32, 16384, 256], P('shard', 'blk'), may hold values from -6 to 6
- dense_tiles: bfloat16 [32, 32, 5, 12, 128, 128], P('shard', 'blk'), may hold values from -0.125 to 0.125
- dense_rows: int32 [32, 32, 5, 12], P('shard', 'blk'), may hold values from 0 to 3, as said below
- dense_cols: int32 [32, 32, 5, 12], P('shard', 'blk'), may hold values from 0 to 3
- send_rows: int32 [32, 32, 32, 16], P('shard', 'blk'), may hold values from 0 to 511
- sparse_target_row: int32 [32, 32, 32, 16], P('shard', 'blk'), may hold values from 0 to 511
- sparse_val: bfloat16 [32, 32, 32, 16], P('shard', 'blk'), may hold values from -4 to 4
- sparse_count: int32 [32, 32, 32], P('shard', 'blk'), may hold values from 1 to 16, as said below
- weight: bfloat16 [256, 256], replicated, may hold values from -0.375 to 0.375
Outputs:
- hidden_out: bfloat16 [32, 16384, 256], P('shard', 'blk')
The draws below stay inside these ranges and needn't reach their ends.
Inputs may be any that keep to these rules, and one draw needn't show every extreme that they name: For each device and source block the 12 pairs (dense_rows, dense_cols) are distinct. `sparse_count`: every device has 16 live slots from the next shard index.
All inputs are finite; a program needn't handle non-finite values.
Results may differ from the reference program's by a relative error of at most 0.015.
Values may be sent and summed in bfloat16 or wider, within the bound.
A program may use at most 32 MiB of HBM per device.

```python
import jax
import jax.numpy as jnp
from jax import lax

FEAT = 256
TILE = 128
SPAN = 2
ROWS_DEV = 512
CAP = 16
TPB = 12
GROUP_ROWS = 16384
N_BLK = 32
N_SHARD = 32


def tile_pattern(key):
    row_tiles = ROWS_DEV // TILE
    scores = jax.random.randint(key, (N_SHARD, N_BLK, 2 * SPAN + 1, row_tiles * row_tiles), 0, 2 ** 20)
    scores = scores * (row_tiles * row_tiles) + jnp.arange(row_tiles * row_tiles, dtype=jnp.int32)
    order = jnp.argsort(scores, axis=-1)[..., :TPB]
    return (order.astype(jnp.int32), row_tiles)


def draw_dense_rows(key, part):
    order, row_tiles = tile_pattern(key)
    return (order // row_tiles).astype(jnp.int32)


def draw_dense_cols(key, part):
    order, row_tiles = tile_pattern(key)
    return (order % row_tiles).astype(jnp.int32)


def draw_sparse_count(key, part):
    key = jax.random.fold_in(key, 7)
    first, second = jax.random.split(key)
    base = jax.random.randint(first, (N_SHARD, N_BLK, N_SHARD), 1, CAP // 2 + 1)
    normal_coefficient = jax.random.randint(second, (N_SHARD, N_BLK, 1), 1, 4)
    counts = jnp.minimum(base * normal_coefficient, CAP)
    receiver = jnp.arange(N_SHARD, dtype=jnp.int32)[:, None, None]
    source = jnp.arange(N_SHARD, dtype=jnp.int32)[None, None, :]
    return jnp.where(source == (receiver + 1) % N_SHARD, CAP, counts).astype(jnp.int32)


def touch_ends(result, stream_key, least, high):
    place = [jax.random.randint(jax.random.fold_in(stream_key, axis), (), 0, length) for axis, length in enumerate(result.shape)]
    longest = result.shape.index(max(result.shape))
    beside = place[:longest] + [(place[longest] + 1) % result.shape[longest]] + place[longest + 1:]
    return result.at[tuple(place)].set(least).at[tuple(beside)].set(high)


def block_levels(rng, extent, cuts, smallest, high):
    def one(dim, blocks):
        steps = jax.random.uniform(jax.random.fold_in(jax.random.fold_in(rng, 6), dim), (blocks,), jnp.float32, smallest / len(cuts), high / len(cuts))
        return jnp.repeat(jnp.exp(steps), extent[dim] // blocks).reshape((-1,) + (1,) * (len(extent) - dim - 1))

    factor_of = one(*cuts[0])
    for cut in cuts[1:]:
        factor_of = factor_of * one(*cut)
    return factor_of


def normal_values(stream_key, dims, deviation, most, pieces=(), held_as=jnp.bfloat16):
    loudness = block_levels(stream_key, dims, pieces, -0.22, 0.18) if pieces else 1.0
    entries = jax.random.normal(stream_key, dims, jnp.float32) * deviation * loudness
    return jnp.minimum(jnp.maximum(entries, -most), most).astype(held_as)


def setup_inputs(seed: int = 0) -> dict:
    arg_keys = jax.random.split(jax.random.key(seed), 10)
    return {
        "features": normal_values(arg_keys[0], (N_SHARD, GROUP_ROWS, FEAT), 1.0, 6.0, ((0, 32), (1, 32))),
        "dense_tiles": normal_values(arg_keys[1], (N_SHARD, N_BLK, 2 * SPAN + 1, TPB, TILE, TILE), ((2 * SPAN + 1) * TPB * TILE * TILE // ROWS_DEV) ** -0.5, 0.125, ((0, 32), (1, 32))),
        "dense_rows": draw_dense_rows(jax.random.fold_in(arg_keys[9], 71), 0),
        "dense_cols": draw_dense_cols(jax.random.fold_in(arg_keys[9], 71), 0),
        "send_rows": touch_ends(jax.random.randint(arg_keys[4], (N_SHARD, N_BLK, N_SHARD, CAP), 0, ROWS_DEV), jax.random.fold_in(arg_keys[4], 1), 0, ROWS_DEV - 1).astype(jnp.int32),
        "sparse_target_row": touch_ends(jax.random.randint(arg_keys[5], (N_SHARD, N_BLK, N_SHARD, CAP), 0, ROWS_DEV), jax.random.fold_in(arg_keys[5], 1), 0, ROWS_DEV - 1).astype(jnp.int32),
        "sparse_val": normal_values(arg_keys[6], (N_SHARD, N_BLK, N_SHARD, CAP), 0.6, 4.0, ((0, 32), (1, 32))),
        "sparse_count": draw_sparse_count(jax.random.fold_in(arg_keys[9], 71), 0),
        "weight": normal_values(arg_keys[8], (FEAT, FEAT), FEAT ** -0.5, 0.375),
    }


def reference(features, dense_tiles, dense_rows, dense_cols, send_rows, sparse_target_row, sparse_val, sparse_count, weight):
    row_tiles = ROWS_DEV // TILE
    reach = 2 * SPAN + 1
    blocks = features.reshape(N_SHARD, N_BLK, row_tiles, TILE, FEAT)
    by_device = features.reshape(N_SHARD, N_BLK, ROWS_DEV, FEAT)

    def device(index):
        group = index // N_BLK
        block = index % N_BLK
        tiles = dense_tiles[group, block].astype(jnp.float32)
        rows = dense_rows[group, block]
        cols = dense_cols[group, block]
        sources = ((block + jnp.arange(reach).astype(jnp.int32) - SPAN) % N_BLK).astype(jnp.int32)
        picked = blocks[group][sources[:, None], cols].astype(jnp.float32)
        prods = jnp.einsum("ctab,ctbf->ctaf", tiles, picked)
        onehot = (rows[..., None] == jnp.arange(row_tiles).astype(jnp.int32)).astype(jnp.float32)
        dense_part = jnp.einsum("ctr,ctaf->raf", onehot, prods).reshape(ROWS_DEV, FEAT)
        lists = send_rows[:, block, group, :]
        received_features = by_device[jnp.arange(N_SHARD).astype(jnp.int32)[:, None], block, lists].astype(jnp.float32)
        live = jnp.arange(CAP).astype(jnp.int32)[None, :] < sparse_count[group, block][:, None]
        values = jnp.where(live, sparse_val[group, block].astype(jnp.float32), jnp.float32(0.0))
        scatter_rows = (sparse_target_row[group, block][..., None] == jnp.arange(ROWS_DEV).astype(jnp.int32)).astype(jnp.float32) * values[..., None]
        sparse_contribution = jnp.einsum("tvz,tvy->zy", scatter_rows, received_features)
        gathered_messages = (dense_part + sparse_contribution).astype(jnp.bfloat16)
        product = jnp.dot(gathered_messages, weight, preferred_element_type=jnp.float32)
        return jnp.maximum(product, 0.0).astype(jnp.bfloat16)

    layer_results = lax.map(device, jnp.arange(N_SHARD * N_BLK).astype(jnp.int32))
    return layer_results.reshape(N_SHARD, N_BLK * ROWS_DEV, FEAT)
```

```python
import functools

import jax
import jax.numpy as jnp
from jax import lax
from jax.experimental import pallas as pl
from jax.experimental.pallas import tpu as pltpu
from jax.sharding import PartitionSpec as P

MESH = pl.DeviceIdType.MESH
F32 = jnp.float32
BF16 = jnp.bfloat16


def iota(shape, axis):
    return lax.broadcasted_iota(jnp.int32, shape, axis)


def mask_of(cond, dtype):
    return jnp.where(cond, F32(1.0), F32(0.0)).astype(dtype)


def kernel(
    n_blk,
    n_shard,
    feats,
    tiles,
    t_rows,
    t_cols,
    send_rows,
    target,
    value,
    count,
    weight,
    out,
    own,
    tiles_v,
    rows_s,
    cols_s,
    send_v,
    target_v,
    value_v,
    count_v,
    weight_v,
    outgoing,
    received,
    arrived,
    acc,
    in_sem,
    tile_sem,
    blk_send,
    blk_recv,
    sh_send,
    sh_recv,
    ready,
    hello,
):
    rows_dev, feat = own.shape
    reach = tiles.shape[2]
    tpb = tiles.shape[3]
    tile = tiles.shape[4]
    span = (reach - 1) // 2
    row_tiles = rows_dev // tile
    slots, peers = send_v.shape
    lanes = peers * slots
    absent = reach * tpb
    me_b = lax.axis_index("blk")
    me_s = lax.axis_index("shard")
    right = lax.rem(me_b + 1, n_blk)
    left = lax.rem(me_b + n_blk - 1, n_blk)

    run = n_blk // 2
    hurry = lax.rem(me_b, run) >= run - 2
    quad = 4 if n_shard % 4 == 0 and n_shard > 4 else 1
    ring = n_shard // quad
    mid = ring // 2
    y, q = me_s // quad, lax.rem(me_s, quad)

    def beside(k, to=None):
        return lax.rem(y + k + ring, ring) * quad + (q if to is None else to)

    def signal(sem, shard):
        pl.semaphore_signal(sem, inc=1, device_id=(me_b, shard), device_id_type=MESH)

    def signal_row(sem, k, cond):
        @pl.when(cond)
        def _():
            for to in range(quad):
                signal(sem, beside(k, to))

    def as_int(cond):
        return jnp.where(cond, 1, 0)

    y_below, y_above = lax.rem(y + ring - 1, ring), lax.rem(y + 1, ring)
    gives_above, gives_below = y < mid, (y == 0) | (y > mid)
    has_below, has_above = y_below < mid, (y_above == 0) | (y_above > mid)
    n_after = quad * (as_int(gives_above) + as_int(gives_below))
    n_before = quad * (as_int(has_below) + as_int(has_above))

    barrier = pltpu.get_barrier_semaphore()
    pl.semaphore_signal(barrier, inc=1, device_id=(left, me_s), device_id_type=MESH)

    @pl.when(hurry)
    def _():
        signal_row(barrier, 1, gives_above)
        signal_row(barrier, -1, gives_below)

    @pl.when(jnp.logical_not(hurry))
    def _():
        def tell(k, c):
            signal(barrier, lax.rem(me_s + k, n_shard))
            return c

        lax.fori_loop(1, n_shard, tell, 0)

    pl.semaphore_wait(barrier, jnp.where(hurry, 1 + n_before, n_shard))

    def answer():
        signal_row(ready.at[0], -1, has_below)
        signal_row(ready.at[0], 1, has_above)

    def meet_near():
        pl.when(n_after > 0)(lambda: pl.semaphore_wait(ready.at[0], n_after))
        for k in (1, -1):
            signal(ready.at[1], beside(k))

    def meet_far():
        pl.semaphore_wait(ready.at[1], 2)
        known, at = 2, 2
        while known < mid:
            for k in (known, -known):
                signal(ready.at[at], beside(k))
            pl.semaphore_wait(ready.at[at], 2)
            known, at = 2 * known, at + 1

    def piece(ref, c):
        return ref.at[pl.ds(c * tile, tile)]

    def send(src, dst, way, c, to):
        copy = pltpu.make_async_remote_copy(
            src_ref=piece(src, c),
            dst_ref=piece(dst, c),
            send_sem=blk_send.at[way, c],
            recv_sem=blk_recv.at[way, c],
            device_id=(to, me_s),
            device_id_type=MESH,
        )
        copy.start()
        return copy

    first = {}
    second = {}
    for c in range(row_tiles):
        first[0, c] = send(feats.at[0], arrived.at[0], 0, c, right)
    pl.semaphore_signal(hello, inc=1, device_id=(right, me_s), device_id_type=MESH)

    def local(src, dst, sem):
        copy = pltpu.make_async_copy(src, dst, sem)
        copy.start()
        return copy

    get_own = local(feats.at[0], own, in_sem.at[0])
    get_send = local(send_rows.at[0, 0], send_v, in_sem.at[1])
    get_rows = local(t_rows.at[0], rows_s, in_sem.at[2])
    get_cols = local(t_cols.at[0], cols_s, in_sem.at[3])
    get_tiles = {
        j: local(tiles.at[0, 0, j], tiles_v.at[pl.ds(j * tpb, tpb)], tile_sem.at[j])
        for j in range(reach)
    }
    get_target = local(target.at[0, 0], target_v, in_sem.at[4])
    get_value = local(value.at[0, 0], value_v, in_sem.at[5])
    get_count = local(count.at[0], count_v, in_sem.at[6])
    get_weight = local(weight, weight_v, in_sem.at[7])

    get_send.wait()
    half = rows_dev // 2
    spread = mask_of(iota((lanes, peers), 0) // slots == iota((lanes, peers), 1), BF16)
    picks = (send_v[...] - half).astype(F32).astype(BF16)
    mine = lax.dot_general(spread, picks, (((1,), (1,)), ((), ())), preferred_element_type=F32)
    mine = jnp.where(iota((lanes, slots), 0) % slots == iota((lanes, slots), 1), mine, 0.0)
    wide = jnp.dot(mine.astype(BF16), jnp.ones((slots, 128), BF16), preferred_element_type=F32)
    pick = jnp.concatenate(
        [
            mask_of(wide == (iota((lanes, 128), 1) + (g * 128 - half)).astype(F32), BF16)
            for g in range(rows_dev // 128)
        ],
        axis=1,
    )
    get_own.wait()
    outgoing[...] = jnp.dot(pick, own[...], preferred_element_type=F32).astype(BF16)

    def give(k):
        to = lax.rem(me_s + k, n_shard)
        pltpu.make_async_remote_copy(
            src_ref=outgoing.at[pl.ds(to * slots, slots)],
            dst_ref=received.at[pl.ds(me_s * slots, slots)],
            send_sem=sh_send,
            recv_sem=sh_recv,
            device_id=(me_b, to),
            device_id_type=MESH,
        ).start()

    def exchange():
        far = n_shard // 2
        give(far)

        def both(i, c):
            give(far - i)
            give(far + i)
            return c

        lax.fori_loop(1, far, both, 0)

    pl.when(hurry)(answer)
    pl.when(jnp.logical_not(hurry))(exchange)

    pl.semaphore_wait(hello, 1)
    for c in range(row_tiles):
        first[1, c] = send(feats.at[0], arrived.at[1], 1, c, left)

    tiles_v[absent] = jnp.zeros((tile, tile), BF16)
    get_rows.wait()
    get_cols.wait()

    def block_matrix(j, cs):
        place = [rows_s[j, 0, t] * row_tiles + cols_s[j, 0, t] for t in range(tpb)]

        def pick_tile(r, c):
            at = jnp.int32(absent)
            for t in range(tpb):
                at = jnp.where(place[t] == r * row_tiles + c, j * tpb + t, at)
            return tiles_v[at]

        return jnp.concatenate(
            [
                jnp.concatenate([pick_tile(r, c) for c in cs], axis=1)
                for r in range(row_tiles)
            ],
            axis=0,
        )

    def times(j, cs, ref):
        x = ref[pl.ds(cs[0] * tile, len(cs) * tile), :]
        return jnp.dot(block_matrix(j, cs), x, preferred_element_type=F32)

    for copy in get_tiles.values():
        copy.wait()
    acc[...] = times(span, range(row_tiles), own)

    get_weight.wait()
    get_target.wait()
    get_value.wait()
    get_count.wait()
    spread_l = mask_of(iota((peers, lanes), 1) // slots == iota((peers, lanes), 0), BF16)
    slot_l = iota((slots, lanes), 1) % slots
    own_slot = slot_l == iota((slots, lanes), 0)

    def along(x):
        wide_x = jnp.dot(x, spread_l, preferred_element_type=F32)
        return jnp.sum(jnp.where(own_slot, wide_x, 0.0), axis=0, keepdims=True)

    target_l = along((target_v[...] - half).astype(F32).astype(BF16))
    value_l = along(value_v[...])
    count_l = jnp.dot(count_v[...].astype(F32).astype(BF16), spread_l, preferred_element_type=F32)
    live = (iota((1, lanes), 1) % slots).astype(F32) < count_l
    value_l = jnp.where(live, value_l, 0.0)
    placing = jnp.where(
        (iota((rows_dev, lanes), 0) - half).astype(F32) == target_l, value_l, 0.0
    ).astype(BF16)

    every = range(row_tiles)
    for c in every:
        first[0, c].wait_recv()
        second[0, c] = send(arrived.at[0], arrived.at[2], 2, c, right)
        first[1, c].wait_recv()
        second[1, c] = send(arrived.at[1], arrived.at[3], 3, c, left)
        if c == row_tiles - 2:
            pl.when(hurry)(meet_near)

    @pl.when(hurry)
    def _():
        meet_far()
        exchange()

    received[pl.ds(me_s * slots, slots), :] = outgoing[pl.ds(me_s * slots, slots), :]
    acc[...] += times(span - 1, every, arrived.at[0])
    acc[...] += times(span + 1, every, arrived.at[1])

    some = pl.ds(0, (n_shard - 1) * slots)
    pltpu.make_async_copy(received.at[some], received.at[some], sh_recv).wait()
    acc[...] += jnp.dot(placing, received[...], preferred_element_type=F32)
    for c in every:
        second[1, c].wait_recv()
    acc[...] += times(span + 2, every, arrived.at[3])

    for c in every:
        second[0, c].wait_recv()
        acc[...] += times(span - 2, [c], arrived.at[2])

    total = acc[...].astype(BF16)
    product = jnp.dot(total, weight_v[...], preferred_element_type=F32)
    out[0] = jnp.maximum(product, 0.0).astype(BF16)

    for copy in list(first.values()) + list(second.values()):
        copy.wait_send()
    pltpu.make_async_copy(outgoing.at[some], outgoing.at[some], sh_send).wait()


def layer(mesh, features, tiles, t_rows, t_cols, send_rows, target, value, count, weight):
    n_blk, n_shard = mesh.shape["blk"], mesh.shape["shard"]
    _, rows_dev, feat = features.shape
    _, _, reach, tpb, tile, _ = tiles.shape
    assert reach == 5 and rows_dev <= 512 and rows_dev % tile == 0
    _, _, peers, slots = send_rows.shape
    row_tiles = rows_dev // tile
    lanes = peers * slots
    dma = pltpu.SemaphoreType.DMA
    flops = 2 * feat * (reach * rows_dev * rows_dev + 2 * rows_dev * lanes + rows_dev * feat)
    return pl.pallas_call(
        functools.partial(kernel, n_blk, n_shard),
        out_shape=pltpu.VMEM((1, rows_dev, feat), BF16),
        in_specs=[pl.BlockSpec(memory_space=pl.ANY)] * 9,
        out_specs=pl.BlockSpec(memory_space=pltpu.VMEM),
        scratch_shapes=[
            pltpu.VMEM((rows_dev, feat), BF16),
            pltpu.VMEM((reach * tpb + 1, tile, tile), BF16),
            pltpu.SMEM((reach, 1, tpb), jnp.int32),
            pltpu.SMEM((reach, 1, tpb), jnp.int32),
            pltpu.VMEM((slots, peers), jnp.int32),
            pltpu.VMEM((slots, peers), jnp.int32),
            pltpu.VMEM((slots, peers), BF16),
            pltpu.VMEM((1, peers), jnp.int32),
            pltpu.VMEM((feat, feat), BF16),
            pltpu.VMEM((lanes, feat), BF16),
            pltpu.VMEM((lanes, feat), BF16),
            pltpu.VMEM((4, rows_dev, feat), BF16),
            pltpu.VMEM((rows_dev, feat), F32),
            dma((8,)),
            dma((reach,)),
            dma((4, row_tiles)),
            dma((4, row_tiles)),
            dma,
            dma,
            pltpu.SemaphoreType.REGULAR((8,)),
            pltpu.SemaphoreType.REGULAR,
        ],
        compiler_params=pltpu.CompilerParams(
            collective_id=0, has_side_effects=True, vmem_limit_bytes=60 * 1024 * 1024
        ),
        cost_estimate=pl.CostEstimate(flops=flops, bytes_accessed=4 << 20, transcendentals=0),
    )(
        features,
        tiles,
        t_rows.transpose(0, 2, 1, 3),
        t_cols.transpose(0, 2, 1, 3),
        send_rows.transpose(0, 1, 3, 2),
        target.transpose(0, 1, 3, 2),
        value.transpose(0, 1, 3, 2),
        count,
        weight,
    )


def solution(mesh):
    return jax.shard_map(
        functools.partial(layer, mesh),
        mesh=mesh,
        in_specs=(
            P("shard", "blk", None),
            P("shard", "blk", None, None, None, None),
            P("shard", "blk", None, None),
            P("shard", "blk", None, None),
            P("shard", "blk", None, None),
            P("shard", "blk", None, None),
            P("shard", "blk", None, None),
            P("shard", "blk", None),
            P(),
        ),
        out_specs=P("shard", "blk", None),
        check_vma=False,
    )
```

```python
import functools

import jax
import jax.numpy as jnp
from jax import lax
from jax.experimental import pallas as pl
from jax.experimental.pallas import tpu as pltpu
from jax.sharding import PartitionSpec as P

MESH = pl.DeviceIdType.MESH
F32 = jnp.float32
BF16 = jnp.bfloat16


def iota(shape, axis):
    return lax.broadcasted_iota(jnp.int32, shape, axis)


def mask_of(cond, dtype):
    return jnp.where(cond, F32(1.0), F32(0.0)).astype(dtype)


def kernel(
    n_blk,
    n_shard,
    feats,
    tiles,
    t_rows,
    t_cols,
    send_rows,
    target,
    value,
    count,
    weight,
    out,
    own,
    tiles_v,
    rows_s,
    cols_s,
    send_v,
    target_v,
    value_v,
    count_v,
    weight_v,
    outgoing,
    received,
    arrived,
    acc,
    in_sem,
    tile_sem,
    blk_send,
    blk_recv,
    sh_send,
    sh_recv,
    ready,
    hello,
):
    rows_dev, feat = own.shape
    reach = tiles.shape[2]
    tpb = tiles.shape[3]
    tile = tiles.shape[4]
    span = (reach - 1) // 2
    row_tiles = rows_dev // tile
    slots, peers = send_v.shape
    lanes = peers * slots
    absent = reach * tpb
    me_b = lax.axis_index("blk")
    me_s = lax.axis_index("shard")
    right = lax.rem(me_b + 1, n_blk)
    left = lax.rem(me_b + n_blk - 1, n_blk)

    run = n_blk // 2
    left3 = lax.rem(me_b + n_blk - 3, n_blk)
    z = lax.rem(me_b, run)
    is_first, is_second, is_third, is_last, by_row = z == 0, z == 1, z == 2, z == run - 1, z == run - 2
    direct = z < run - 2
    quad = 4 if n_shard % 4 == 0 and n_shard > 4 else 1
    ring = n_shard // quad
    mid = ring // 2
    y, q = me_s // quad, lax.rem(me_s, quad)

    def beside(k, to=None):
        return lax.rem(y + k + ring, ring) * quad + (q if to is None else to)

    def signal(sem, shard):
        pl.semaphore_signal(sem, inc=1, device_id=(me_b, shard), device_id_type=MESH)

    def signal_row(sem, k, cond):
        @pl.when(cond)
        def _():
            for to in range(quad):
                signal(sem, beside(k, to))

    def as_int(cond):
        return jnp.where(cond, 1, 0)

    y_below, y_above = lax.rem(y + ring - 1, ring), lax.rem(y + 1, ring)
    gives_above, gives_below = y < mid, (y == 0) | (y > mid)
    has_below, has_above = y_below < mid, (y_above == 0) | (y_above > mid)
    n_after = quad * (as_int(gives_above) + as_int(gives_below))
    n_before = quad * (as_int(has_below) + as_int(has_above))

    barrier = pltpu.get_barrier_semaphore()
    pl.semaphore_signal(barrier, inc=1, device_id=(left, me_s), device_id_type=MESH)

    @pl.when(by_row)
    def _():
        signal_row(barrier, 1, gives_above)
        signal_row(barrier, -1, gives_below)

    def tell_all(sem):
        def tell(k, c):
            signal(sem, lax.rem(me_s + k, n_shard))
            return c

        lax.fori_loop(1, n_shard, tell, 0)

    straggler = (me_b == 0) & (me_s == 0)
    without = (me_b == 0) & (me_s != 0)
    pl.when(direct & jnp.logical_not(straggler))(lambda: tell_all(barrier))
    needed = jnp.where(without, n_shard - 1, n_shard)
    pl.semaphore_wait(barrier, jnp.where(direct, needed, jnp.where(by_row, 1 + n_before, 1)))
    pl.when(straggler)(lambda: tell_all(ready.at[4]))

    def answer():
        signal_row(ready.at[0], -1, has_below)
        signal_row(ready.at[0], 1, has_above)

    def meet_near():
        pl.when(n_after > 0)(lambda: pl.semaphore_wait(ready.at[0], n_after))
        for k in (1, -1):
            signal(ready.at[1], beside(k))

    def meet_far():
        pl.semaphore_wait(ready.at[1], 2)
        known, at = 2, 2
        while known < mid:
            for k in (known, -known):
                signal(ready.at[at], beside(k))
            pl.semaphore_wait(ready.at[at], 2)
            known, at = 2 * known, at + 1

    def piece(ref, c):
        return ref.at[pl.ds(c * tile, tile)]

    def pieces(src, dst, way, sent, c, to):
        return pltpu.make_async_remote_copy(
            src_ref=piece(src, c),
            dst_ref=piece(dst, c),
            send_sem=blk_send.at[sent, c],
            recv_sem=blk_recv.at[way, c],
            device_id=(to, me_s),
            device_id_type=MESH,
        )

    def send(src, dst, way, c, to):
        copy = pieces(src, dst, way, way, c, to)
        copy.start()
        return copy

    first = {}
    second = {}
    for c in range(row_tiles):
        first[0, c] = send(feats.at[0], arrived.at[0], 0, c, right)
    pl.semaphore_signal(hello, inc=1, device_id=(right, me_s), device_id_type=MESH)

    def local(src, dst, sem):
        copy = pltpu.make_async_copy(src, dst, sem)
        copy.start()
        return copy

    get_own = local(feats.at[0], own, in_sem.at[0])
    get_send = local(send_rows.at[0, 0], send_v, in_sem.at[1])
    get_rows = local(t_rows.at[0], rows_s, in_sem.at[2])
    get_cols = local(t_cols.at[0], cols_s, in_sem.at[3])
    get_tiles = {
        j: local(tiles.at[0, 0, j], tiles_v.at[pl.ds(j * tpb, tpb)], tile_sem.at[j])
        for j in range(reach)
    }
    get_target = local(target.at[0, 0], target_v, in_sem.at[4])
    get_value = local(value.at[0, 0], value_v, in_sem.at[5])
    get_count = local(count.at[0], count_v, in_sem.at[6])
    get_weight = local(weight, weight_v, in_sem.at[7])

    half = rows_dev // 2

    def gather():
        spread = mask_of(iota((lanes, peers), 0) // slots == iota((lanes, peers), 1), BF16)
        picks = (send_v[...] - half).astype(F32).astype(BF16)
        mine = lax.dot_general(spread, picks, (((1,), (1,)), ((), ())), preferred_element_type=F32)
        mine = jnp.where(iota((lanes, slots), 0) % slots == iota((lanes, slots), 1), mine, 0.0)
        wide = jnp.dot(mine.astype(BF16), jnp.ones((slots, 128), BF16), preferred_element_type=F32)
        pick = jnp.concatenate(
            [
                mask_of(wide == (iota((lanes, 128), 1) + (g * 128 - half)).astype(F32), BF16)
                for g in range(rows_dev // 128)
            ],
            axis=1,
        )
        outgoing[...] = jnp.dot(pick, own[...], preferred_element_type=F32).astype(BF16)

    def give(k):
        to = lax.rem(me_s + k, n_shard)
        pltpu.make_async_remote_copy(
            src_ref=outgoing.at[pl.ds(to * slots, slots)],
            dst_ref=received.at[pl.ds(me_s * slots, slots)],
            send_sem=sh_send,
            recv_sem=sh_recv,
            device_id=(me_b, to),
            device_id_type=MESH,
        ).start()

    def exchange():
        gather()
        far = n_shard // 2

        def but(k):
            skip = without & (lax.rem(me_s + k, n_shard) == 0)
            pl.when(jnp.logical_not(skip))(lambda: give(k))

        but(far)

        def both(i, c):
            but(far - i)
            but(far + i)
            return c

        lax.fori_loop(1, far, both, 0)

    pl.when(by_row)(answer)
    get_send.wait()
    get_own.wait()
    pl.when(direct)(exchange)

    pl.semaphore_wait(hello, 1)

    @pl.when(without)
    def _():
        pl.semaphore_wait(ready.at[4], 1)
        give(n_shard - me_s)

    for c in range(row_tiles):
        first[1, c] = send(feats.at[0], arrived.at[1], 1, c, left)
    pl.when(is_first)(lambda: tell_all(ready.at[6]))

    every = range(row_tiles)
    for c in every:
        first[0, c].wait_recv()
        second[0, c] = send(arrived.at[0], arrived.at[2], 2, c, right)
        first[1, c].wait_recv()
        second[1, c] = pieces(arrived.at[1], arrived.at[3], 3, 3, c, left)
        pl.when(jnp.logical_not(is_first))(second[1, c].start)
        if c == row_tiles - 2:
            pl.when(by_row)(meet_near)

    third = [pieces(arrived.at[0], arrived.at[3], 3, 4, c, left3) for c in every]

    @pl.when(is_third)
    def _():
        pl.semaphore_wait(ready.at[5], 1)
        for copy in third:
            copy.start()

    @pl.when(by_row)
    def _():
        meet_far()
        exchange()

    @pl.when(is_last)
    def _():
        pl.semaphore_wait(ready.at[7], 1)
        exchange()

    tiles_v[absent] = jnp.zeros((tile, tile), BF16)
    get_rows.wait()
    get_cols.wait()

    def block_matrix(j, cs):
        place = [rows_s[j, 0, t] * row_tiles + cols_s[j, 0, t] for t in range(tpb)]

        def pick_tile(r, c):
            at = jnp.int32(absent)
            for t in range(tpb):
                at = jnp.where(place[t] == r * row_tiles + c, j * tpb + t, at)
            return tiles_v[at]

        return jnp.concatenate(
            [
                jnp.concatenate([pick_tile(r, c) for c in cs], axis=1)
                for r in range(row_tiles)
            ],
            axis=0,
        )

    def times(j, cs, ref):
        x = ref[pl.ds(cs[0] * tile, len(cs) * tile), :]
        return jnp.dot(block_matrix(j, cs), x, preferred_element_type=F32)

    for copy in get_tiles.values():
        copy.wait()
    acc[...] = times(span, range(row_tiles), own)

    get_weight.wait()
    get_target.wait()
    get_value.wait()
    get_count.wait()
    spread_l = mask_of(iota((peers, lanes), 1) // slots == iota((peers, lanes), 0), BF16)
    slot_l = iota((slots, lanes), 1) % slots
    own_slot = slot_l == iota((slots, lanes), 0)

    def along(x):
        wide_x = jnp.dot(x, spread_l, preferred_element_type=F32)
        return jnp.sum(jnp.where(own_slot, wide_x, 0.0), axis=0, keepdims=True)

    target_l = along((target_v[...] - half).astype(F32).astype(BF16))
    value_l = along(value_v[...])
    count_l = jnp.dot(count_v[...].astype(F32).astype(BF16), spread_l, preferred_element_type=F32)
    live = (iota((1, lanes), 1) % slots).astype(F32) < count_l
    value_l = jnp.where(live, value_l, 0.0)
    placing = jnp.where(
        (iota((rows_dev, lanes), 0) - half).astype(F32) == target_l, value_l, 0.0
    ).astype(BF16)

    received[pl.ds(me_s * slots, slots), :] = outgoing[pl.ds(me_s * slots, slots), :]
    acc[...] += times(span - 1, every, arrived.at[0])
    acc[...] += times(span + 1, every, arrived.at[1])

    some = pl.ds(0, (n_shard - 1) * slots)
    pltpu.make_async_copy(received.at[some], received.at[some], sh_recv).wait()
    acc[...] += jnp.dot(placing, received[...], preferred_element_type=F32)
    for c in every:
        second[1, c].wait_recv()
    acc[...] += times(span + 2, every, arrived.at[3])

    for c in every:
        second[0, c].wait_recv()
        if c == 0:
            @pl.when(is_second)
            def _():
                pl.semaphore_signal(ready.at[5], inc=1, device_id=(right, me_s), device_id_type=MESH)

        if c == row_tiles - 2:
            @pl.when(is_first)
            def _():
                pl.semaphore_wait(ready.at[6], n_shard - 1)
                pl.semaphore_signal(ready.at[7], inc=1, device_id=(left, me_s), device_id_type=MESH)
        acc[...] += times(span - 2, [c], arrived.at[2])

    total = acc[...].astype(BF16)
    product = jnp.dot(total, weight_v[...], preferred_element_type=F32)
    out[0] = jnp.maximum(product, 0.0).astype(BF16)

    for copy in list(first.values()) + [second[0, c] for c in every]:
        copy.wait_send()

    @pl.when(jnp.logical_not(is_first))
    def _():
        for c in every:
            second[1, c].wait_send()

    @pl.when(is_third)
    def _():
        for copy in third:
            copy.wait_send()

    pltpu.make_async_copy(outgoing.at[some], outgoing.at[some], sh_send).wait()


def layer(mesh, features, tiles, t_rows, t_cols, send_rows, target, value, count, weight):
    n_blk, n_shard = mesh.shape["blk"], mesh.shape["shard"]
    _, rows_dev, feat = features.shape
    _, _, reach, tpb, tile, _ = tiles.shape
    assert reach == 5 and rows_dev <= 512 and rows_dev % tile == 0
    _, _, peers, slots = send_rows.shape
    row_tiles = rows_dev // tile
    lanes = peers * slots
    dma = pltpu.SemaphoreType.DMA
    flops = 2 * feat * (reach * rows_dev * rows_dev + 2 * rows_dev * lanes + rows_dev * feat)
    return pl.pallas_call(
        functools.partial(kernel, n_blk, n_shard),
        out_shape=pltpu.VMEM((1, rows_dev, feat), BF16),
        in_specs=[pl.BlockSpec(memory_space=pl.ANY)] * 9,
        out_specs=pl.BlockSpec(memory_space=pltpu.VMEM),
        scratch_shapes=[
            pltpu.VMEM((rows_dev, feat), BF16),
            pltpu.VMEM((reach * tpb + 1, tile, tile), BF16),
            pltpu.SMEM((reach, 1, tpb), jnp.int32),
            pltpu.SMEM((reach, 1, tpb), jnp.int32),
            pltpu.VMEM((slots, peers), jnp.int32),
            pltpu.VMEM((slots, peers), jnp.int32),
            pltpu.VMEM((slots, peers), BF16),
            pltpu.VMEM((1, peers), jnp.int32),
            pltpu.VMEM((feat, feat), BF16),
            pltpu.VMEM((lanes, feat), BF16),
            pltpu.VMEM((lanes, feat), BF16),
            pltpu.VMEM((4, rows_dev, feat), BF16),
            pltpu.VMEM((rows_dev, feat), F32),
            dma((8,)),
            dma((reach,)),
            dma((5, row_tiles)),
            dma((4, row_tiles)),
            dma,
            dma,
            pltpu.SemaphoreType.REGULAR((8,)),
            pltpu.SemaphoreType.REGULAR,
        ],
        compiler_params=pltpu.CompilerParams(
            collective_id=0, has_side_effects=True, vmem_limit_bytes=60 * 1024 * 1024
        ),
        cost_estimate=pl.CostEstimate(flops=flops, bytes_accessed=4 << 20, transcendentals=0),
    )(
        features,
        tiles,
        t_rows.transpose(0, 2, 1, 3),
        t_cols.transpose(0, 2, 1, 3),
        send_rows.transpose(0, 1, 3, 2),
        target.transpose(0, 1, 3, 2),
        value.transpose(0, 1, 3, 2),
        count,
        weight,
    )


def solution(mesh):
    return jax.shard_map(
        functools.partial(layer, mesh),
        mesh=mesh,
        in_specs=(
            P("shard", "blk", None),
            P("shard", "blk", None, None, None, None),
            P("shard", "blk", None, None),
            P("shard", "blk", None, None),
            P("shard", "blk", None, None),
            P("shard", "blk", None, None),
            P("shard", "blk", None, None),
            P("shard", "blk", None),
            P(),
        ),
        out_specs=P("shard", "blk", None),
        check_vma=False,
    )
```

```python
import functools

import jax
import jax.numpy as jnp
from jax import lax
from jax.experimental import pallas as pl
from jax.experimental.pallas import tpu as pltpu
from jax.sharding import PartitionSpec as P

MESH = pl.DeviceIdType.MESH
F32 = jnp.float32
BF16 = jnp.bfloat16


def iota(shape, axis):
    return lax.broadcasted_iota(jnp.int32, shape, axis)


def mask_of(cond, dtype):
    return jnp.where(cond, F32(1.0), F32(0.0)).astype(dtype)


def kernel(
    n_blk,
    n_shard,
    feats,
    tiles,
    t_rows,
    t_cols,
    send_rows,
    target,
    value,
    count,
    weight,
    out,
    own,
    tiles_v,
    rows_s,
    cols_s,
    send_v,
    target_v,
    value_v,
    count_v,
    weight_v,
    outgoing,
    received,
    arrived,
    acc,
    in_sem,
    tile_sem,
    blk_send,
    blk_recv,
    sh_send,
    sh_recv,
    ready,
    hello,
):
    rows_dev, feat = own.shape
    reach = tiles.shape[2]
    tpb = tiles.shape[3]
    tile = tiles.shape[4]
    span = (reach - 1) // 2
    row_tiles = rows_dev // tile
    slots, peers = send_v.shape
    lanes = peers * slots
    absent = reach * tpb
    me_b = lax.axis_index("blk")
    me_s = lax.axis_index("shard")
    right = lax.rem(me_b + 1, n_blk)
    left = lax.rem(me_b + n_blk - 1, n_blk)

    run = n_blk // 2
    left3 = lax.rem(me_b + n_blk - 3, n_blk)
    z = lax.rem(me_b, run)
    is_first, is_second, is_third, is_last, is_late = z == 0, z == 1, z == 2, z == run - 1, z == run - 2
    direct = z < run - 2
    before_late = z == run - 3
    def signal(sem, shard):
        pl.semaphore_signal(sem, inc=1, device_id=(me_b, shard), device_id_type=MESH)

    barrier = pltpu.get_barrier_semaphore()
    pl.semaphore_signal(barrier, inc=1, device_id=(left, me_s), device_id_type=MESH)

    def tell_all(sem):
        def tell(k, c):
            signal(sem, lax.rem(me_s + k, n_shard))
            return c

        lax.fori_loop(1, n_shard, tell, 0)

    straggler = (me_b == 0) & (me_s == 0)
    without = (me_b == 0) & (me_s != 0)
    pl.when(direct & jnp.logical_not(straggler))(lambda: tell_all(barrier))
    needed = jnp.where(without, n_shard - 1, n_shard)
    pl.semaphore_wait(barrier, jnp.where(direct, needed, 1))
    pl.when(straggler)(lambda: tell_all(ready.at[3]))

    pl.when(before_late)(lambda: tell_all(ready.at[0]))

    def piece(ref, c):
        return ref.at[pl.ds(c * tile, tile)]

    def pieces(src, dst, way, sent, c, to):
        return pltpu.make_async_remote_copy(
            src_ref=piece(src, c),
            dst_ref=piece(dst, c),
            send_sem=blk_send.at[sent, c],
            recv_sem=blk_recv.at[way, c],
            device_id=(to, me_s),
            device_id_type=MESH,
        )

    def send(src, dst, way, c, to):
        copy = pieces(src, dst, way, way, c, to)
        copy.start()
        return copy

    first = {}
    second = {}
    for c in range(row_tiles):
        first[0, c] = send(feats.at[0], arrived.at[0], 0, c, right)
        if c == 0:
            pl.semaphore_signal(hello, inc=1, device_id=(right, me_s), device_id_type=MESH)

    def local(src, dst, sem):
        copy = pltpu.make_async_copy(src, dst, sem)
        copy.start()
        return copy

    get_own = local(feats.at[0], own, in_sem.at[0])
    get_send = local(send_rows.at[0, 0], send_v, in_sem.at[1])
    get_rows = local(t_rows.at[0], rows_s, in_sem.at[2])
    get_cols = local(t_cols.at[0], cols_s, in_sem.at[3])
    get_tiles = {
        j: local(tiles.at[0, 0, j], tiles_v.at[pl.ds(j * tpb, tpb)], tile_sem.at[j])
        for j in range(reach)
    }
    get_target = local(target.at[0, 0], target_v, in_sem.at[4])
    get_value = local(value.at[0, 0], value_v, in_sem.at[5])
    get_count = local(count.at[0], count_v, in_sem.at[6])
    get_weight = local(weight, weight_v, in_sem.at[7])

    half = rows_dev // 2

    def gather():
        spread = mask_of(iota((lanes, peers), 0) // slots == iota((lanes, peers), 1), BF16)
        picks = (send_v[...] - half).astype(F32).astype(BF16)
        mine = lax.dot_general(spread, picks, (((1,), (1,)), ((), ())), preferred_element_type=F32)
        mine = jnp.where(iota((lanes, slots), 0) % slots == iota((lanes, slots), 1), mine, 0.0)
        wide = jnp.dot(mine.astype(BF16), jnp.ones((slots, 128), BF16), preferred_element_type=F32)
        pick = jnp.concatenate(
            [
                mask_of(wide == (iota((lanes, 128), 1) + (g * 128 - half)).astype(F32), BF16)
                for g in range(rows_dev // 128)
            ],
            axis=1,
        )
        outgoing[...] = jnp.dot(pick, own[...], preferred_element_type=F32).astype(BF16)

    def give(k):
        to = lax.rem(me_s + k, n_shard)
        pltpu.make_async_remote_copy(
            src_ref=outgoing.at[pl.ds(to * slots, slots)],
            dst_ref=received.at[pl.ds(me_s * slots, slots)],
            send_sem=sh_send,
            recv_sem=sh_recv,
            device_id=(me_b, to),
            device_id_type=MESH,
        ).start()

    def exchange():
        gather()
        far = n_shard // 2

        def but(k):
            skip = without & (lax.rem(me_s + k, n_shard) == 0)
            pl.when(jnp.logical_not(skip))(lambda: give(k))

        but(far)

        def both(i, c):
            but(far - i)
            but(far + i)
            return c

        lax.fori_loop(1, far, both, 0)

    get_send.wait()
    get_own.wait()
    pl.when(direct)(exchange)

    pl.semaphore_wait(hello, 1)

    @pl.when(without)
    def _():
        pl.semaphore_wait(ready.at[3], 1)
        give(n_shard - me_s)

    pl.when(is_first)(lambda: tell_all(ready.at[1]))

    for c in range(row_tiles):
        first[1, c] = send(feats.at[0], arrived.at[1], 1, c, left)

    every = range(row_tiles)
    for c in every:
        first[0, c].wait_recv()
        second[0, c] = send(arrived.at[0], arrived.at[2], 2, c, right)
        first[1, c].wait_recv()
        second[1, c] = pieces(arrived.at[1], arrived.at[3], 3, 3, c, left)
        pl.when(jnp.logical_not(is_first))(second[1, c].start)

    third = [pieces(arrived.at[0], arrived.at[3], 3, 4, c, left3) for c in every]

    @pl.when(is_second)
    def _():
        second[0, 0].wait_recv()
        pl.semaphore_signal(ready.at[4], inc=1, device_id=(right, me_s), device_id_type=MESH)

    @pl.when(is_third)
    def _():
        pl.semaphore_wait(ready.at[4], 1)
        for copy in third:
            copy.start()

    @pl.when(before_late)
    def _():
        pl.semaphore_wait(ready.at[0], n_shard - 1)
        pl.semaphore_signal(ready.at[2], inc=1, device_id=(right, me_s), device_id_type=MESH)

    @pl.when(is_late | is_last)
    def _():
        pl.semaphore_wait(ready.at[2], 1)
        exchange()

    tiles_v[absent] = jnp.zeros((tile, tile), BF16)
    get_rows.wait()
    get_cols.wait()

    def block_matrix(j, cs):
        place = [rows_s[j, 0, t] * row_tiles + cols_s[j, 0, t] for t in range(tpb)]

        def pick_tile(r, c):
            at = jnp.int32(absent)
            for t in range(tpb):
                at = jnp.where(place[t] == r * row_tiles + c, j * tpb + t, at)
            return tiles_v[at]

        return jnp.concatenate(
            [
                jnp.concatenate([pick_tile(r, c) for c in cs], axis=1)
                for r in range(row_tiles)
            ],
            axis=0,
        )

    def times(j, cs, ref):
        x = ref[pl.ds(cs[0] * tile, len(cs) * tile), :]
        return jnp.dot(block_matrix(j, cs), x, preferred_element_type=F32)

    for copy in get_tiles.values():
        copy.wait()
    acc[...] = times(span, range(row_tiles), own)

    get_weight.wait()
    get_target.wait()
    get_value.wait()
    get_count.wait()
    spread_l = mask_of(iota((peers, lanes), 1) // slots == iota((peers, lanes), 0), BF16)
    slot_l = iota((slots, lanes), 1) % slots
    own_slot = slot_l == iota((slots, lanes), 0)

    def along(x):
        wide_x = jnp.dot(x, spread_l, preferred_element_type=F32)
        return jnp.sum(jnp.where(own_slot, wide_x, 0.0), axis=0, keepdims=True)

    target_l = along((target_v[...] - half).astype(F32).astype(BF16))
    value_l = along(value_v[...])
    count_l = jnp.dot(count_v[...].astype(F32).astype(BF16), spread_l, preferred_element_type=F32)
    live = (iota((1, lanes), 1) % slots).astype(F32) < count_l
    value_l = jnp.where(live, value_l, 0.0)
    placing = jnp.where(
        (iota((rows_dev, lanes), 0) - half).astype(F32) == target_l, value_l, 0.0
    ).astype(BF16)

    received[pl.ds(me_s * slots, slots), :] = outgoing[pl.ds(me_s * slots, slots), :]
    acc[...] += times(span - 1, every, arrived.at[0])
    acc[...] += times(span + 1, every, arrived.at[1])

    some = pl.ds(0, (n_shard - 1) * slots)
    pltpu.make_async_copy(received.at[some], received.at[some], sh_recv).wait()
    acc[...] += jnp.dot(placing, received[...], preferred_element_type=F32)
    for c in every:
        second[1, c].wait_recv()
    acc[...] += times(span + 2, every, arrived.at[3])

    for c in every:
        if c == 0:
            pl.when(jnp.logical_not(is_second))(second[0, c].wait_recv)
        else:
            second[0, c].wait_recv()
        if c == row_tiles - 2:
            @pl.when(is_first)
            def _():
                pl.semaphore_wait(ready.at[1], n_shard - 1)
                pl.semaphore_signal(ready.at[2], inc=1, device_id=(left, me_s), device_id_type=MESH)
        acc[...] += times(span - 2, [c], arrived.at[2])

    total = acc[...].astype(BF16)
    product = jnp.dot(total, weight_v[...], preferred_element_type=F32)
    out[0] = jnp.maximum(product, 0.0).astype(BF16)

    for copy in list(first.values()) + [second[0, c] for c in every]:
        copy.wait_send()

    @pl.when(jnp.logical_not(is_first))
    def _():
        for c in every:
            second[1, c].wait_send()

    @pl.when(is_third)
    def _():
        for copy in third:
            copy.wait_send()

    pltpu.make_async_copy(outgoing.at[some], outgoing.at[some], sh_send).wait()


def layer(mesh, features, tiles, t_rows, t_cols, send_rows, target, value, count, weight):
    n_blk, n_shard = mesh.shape["blk"], mesh.shape["shard"]
    _, rows_dev, feat = features.shape
    _, _, reach, tpb, tile, _ = tiles.shape
    assert reach == 5 and rows_dev <= 512 and rows_dev % tile == 0
    _, _, peers, slots = send_rows.shape
    row_tiles = rows_dev // tile
    lanes = peers * slots
    dma = pltpu.SemaphoreType.DMA
    flops = 2 * feat * (reach * rows_dev * rows_dev + 2 * rows_dev * lanes + rows_dev * feat)
    return pl.pallas_call(
        functools.partial(kernel, n_blk, n_shard),
        out_shape=pltpu.VMEM((1, rows_dev, feat), BF16),
        in_specs=[pl.BlockSpec(memory_space=pl.ANY)] * 9,
        out_specs=pl.BlockSpec(memory_space=pltpu.VMEM),
        scratch_shapes=[
            pltpu.VMEM((rows_dev, feat), BF16),
            pltpu.VMEM((reach * tpb + 1, tile, tile), BF16),
            pltpu.SMEM((reach, 1, tpb), jnp.int32),
            pltpu.SMEM((reach, 1, tpb), jnp.int32),
            pltpu.VMEM((slots, peers), jnp.int32),
            pltpu.VMEM((slots, peers), jnp.int32),
            pltpu.VMEM((slots, peers), BF16),
            pltpu.VMEM((1, peers), jnp.int32),
            pltpu.VMEM((feat, feat), BF16),
            pltpu.VMEM((lanes, feat), BF16),
            pltpu.VMEM((lanes, feat), BF16),
            pltpu.VMEM((4, rows_dev, feat), BF16),
            pltpu.VMEM((rows_dev, feat), F32),
            dma((8,)),
            dma((reach,)),
            dma((5, row_tiles)),
            dma((4, row_tiles)),
            dma,
            dma,
            pltpu.SemaphoreType.REGULAR((5,)),
            pltpu.SemaphoreType.REGULAR,
        ],
        compiler_params=pltpu.CompilerParams(
            collective_id=0, has_side_effects=True, vmem_limit_bytes=60 * 1024 * 1024
        ),
        cost_estimate=pl.CostEstimate(flops=flops, bytes_accessed=4 << 20, transcendentals=0),
    )(
        features,
        tiles,
        t_rows.transpose(0, 2, 1, 3),
        t_cols.transpose(0, 2, 1, 3),
        send_rows.transpose(0, 1, 3, 2),
        target.transpose(0, 1, 3, 2),
        value.transpose(0, 1, 3, 2),
        count,
        weight,
    )


def solution(mesh):
    return jax.shard_map(
        functools.partial(layer, mesh),
        mesh=mesh,
        in_specs=(
            P("shard", "blk", None),
            P("shard", "blk", None, None, None, None),
            P("shard", "blk", None, None),
            P("shard", "blk", None, None),
            P("shard", "blk", None, None),
            P("shard", "blk", None, None),
            P("shard", "blk", None, None),
            P("shard", "blk", None),
            P(),
        ),
        out_specs=P("shard", "blk", None),
        check_vma=False,
    )
```

```python
import functools

import jax
import jax.numpy as jnp
from jax import lax
from jax.experimental import pallas as pl
from jax.experimental.pallas import tpu as pltpu
from jax.sharding import PartitionSpec as P

MESH = pl.DeviceIdType.MESH
F32 = jnp.float32
BF16 = jnp.bfloat16


def iota(shape, axis):
    return lax.broadcasted_iota(jnp.int32, shape, axis)


def mask_of(cond, dtype):
    return jnp.where(cond, F32(1.0), F32(0.0)).astype(dtype)


def kernel(
    n_blk,
    n_shard,
    feats,
    tiles,
    t_rows,
    t_cols,
    send_rows,
    target,
    value,
    count,
    weight,
    out,
    own,
    tiles_v,
    rows_s,
    cols_s,
    send_v,
    target_v,
    value_v,
    count_v,
    weight_v,
    outgoing,
    received,
    arrived,
    acc,
    in_sem,
    tile_sem,
    blk_send,
    blk_recv,
    sh_send,
    sh_recv,
    ready,
    hello,
):
    rows_dev, feat = own.shape
    reach = tiles.shape[2]
    tpb = tiles.shape[3]
    tile = tiles.shape[4]
    span = (reach - 1) // 2
    row_tiles = rows_dev // tile
    slots, peers = send_v.shape
    lanes = peers * slots
    absent = reach * tpb
    me_b = lax.axis_index("blk")
    me_s = lax.axis_index("shard")
    right = lax.rem(me_b + 1, n_blk)
    left = lax.rem(me_b + n_blk - 1, n_blk)

    run = n_blk // 2
    left3 = lax.rem(me_b + n_blk - 3, n_blk)
    z = lax.rem(me_b, run)
    is_first, is_second, is_third, is_last, is_late = z == 0, z == 1, z == 2, z == run - 1, z == run - 2
    direct = z < run - 2
    before_late = z == run - 3
    def signal(sem, shard):
        pl.semaphore_signal(sem, inc=1, device_id=(me_b, shard), device_id_type=MESH)

    barrier = pltpu.get_barrier_semaphore()
    pl.semaphore_signal(barrier, inc=1, device_id=(left, me_s), device_id_type=MESH)

    def tell_all(sem):
        def tell(k, c):
            signal(sem, lax.rem(me_s + k, n_shard))
            return c

        lax.fori_loop(1, n_shard, tell, 0)

    straggler = (me_b == 0) & (me_s == 0)
    without = (me_b == 0) & (me_s != 0)
    pl.when(direct & jnp.logical_not(straggler))(lambda: tell_all(barrier))
    needed = jnp.where(without, n_shard - 1, n_shard)
    pl.semaphore_wait(barrier, jnp.where(direct, needed, 1))
    pl.when(straggler)(lambda: tell_all(ready.at[3]))

    pl.when(before_late)(lambda: tell_all(ready.at[0]))

    def piece(ref, c):
        return ref.at[pl.ds(c * tile, tile)]

    def pieces(src, dst, way, sent, c, to):
        return pltpu.make_async_remote_copy(
            src_ref=piece(src, c),
            dst_ref=piece(dst, c),
            send_sem=blk_send.at[sent, c],
            recv_sem=blk_recv.at[way, c],
            device_id=(to, me_s),
            device_id_type=MESH,
        )

    def send(src, dst, way, c, to):
        copy = pieces(src, dst, way, way, c, to)
        copy.start()
        return copy

    first = {}
    second = {}
    for c in range(row_tiles):
        first[0, c] = send(feats.at[0], arrived.at[0], 0, c, right)
        if c == 0:
            pl.semaphore_signal(hello, inc=1, device_id=(right, me_s), device_id_type=MESH)

    def local(src, dst, sem):
        copy = pltpu.make_async_copy(src, dst, sem)
        copy.start()
        return copy

    get_own = local(feats.at[0], own, in_sem.at[0])
    get_send = local(send_rows.at[0, 0], send_v, in_sem.at[1])
    get_rows = local(t_rows.at[0], rows_s, in_sem.at[2])
    get_cols = local(t_cols.at[0], cols_s, in_sem.at[3])
    get_tiles = {
        j: local(tiles.at[0, 0, j], tiles_v.at[pl.ds(j * tpb, tpb)], tile_sem.at[j])
        for j in range(reach)
    }
    get_target = local(target.at[0, 0], target_v, in_sem.at[4])
    get_value = local(value.at[0, 0], value_v, in_sem.at[5])
    get_count = local(count.at[0], count_v, in_sem.at[6])
    get_weight = local(weight, weight_v, in_sem.at[7])

    half = rows_dev // 2

    def gather():
        spread = mask_of(iota((lanes, peers), 0) // slots == iota((lanes, peers), 1), BF16)
        picks = (send_v[...] - half).astype(F32).astype(BF16)
        mine = lax.dot_general(spread, picks, (((1,), (1,)), ((), ())), preferred_element_type=F32)
        mine = jnp.where(iota((lanes, slots), 0) % slots == iota((lanes, slots), 1), mine, 0.0)
        wide = jnp.dot(mine.astype(BF16), jnp.ones((slots, 128), BF16), preferred_element_type=F32)
        pick = jnp.concatenate(
            [
                mask_of(wide == (iota((lanes, 128), 1) + (g * 128 - half)).astype(F32), BF16)
                for g in range(rows_dev // 128)
            ],
            axis=1,
        )
        outgoing[...] = jnp.dot(pick, own[...], preferred_element_type=F32).astype(BF16)

    def give(k):
        to = lax.rem(me_s + k, n_shard)
        pltpu.make_async_remote_copy(
            src_ref=outgoing.at[pl.ds(to * slots, slots)],
            dst_ref=received.at[pl.ds(me_s * slots, slots)],
            send_sem=sh_send,
            recv_sem=sh_recv,
            device_id=(me_b, to),
            device_id_type=MESH,
        ).start()

    def exchange():
        gather()
        far = n_shard // 2

        def but(k):
            skip = without & (lax.rem(me_s + k, n_shard) == 0)
            pl.when(jnp.logical_not(skip))(lambda: give(k))

        but(far)

        def both(i, c):
            but(far - i)
            but(far + i)
            return c

        lax.fori_loop(1, far, both, 0)

    get_send.wait()
    get_own.wait()
    pl.when(direct)(exchange)

    @pl.when(without)
    def _():
        pl.semaphore_wait(ready.at[3], 1)
        give(n_shard - me_s)

    pl.semaphore_wait(hello, 1)

    pl.when(is_first)(lambda: tell_all(ready.at[1]))

    for c in range(row_tiles):
        first[1, c] = send(feats.at[0], arrived.at[1], 1, c, left)

    every = range(row_tiles)
    for c in every:
        first[0, c].wait_recv()
        second[0, c] = send(arrived.at[0], arrived.at[2], 2, c, right)
        first[1, c].wait_recv()
        second[1, c] = pieces(arrived.at[1], arrived.at[3], 3, 3, c, left)
        pl.when(jnp.logical_not(is_first))(second[1, c].start)

    third = [pieces(arrived.at[0], arrived.at[3], 3, 4, c, left3) for c in every]

    @pl.when(is_second)
    def _():
        second[0, 0].wait_recv()
        pl.semaphore_signal(ready.at[4], inc=1, device_id=(right, me_s), device_id_type=MESH)

    @pl.when(is_third)
    def _():
        pl.semaphore_wait(ready.at[4], 1)
        for copy in third:
            copy.start()

    @pl.when(before_late)
    def _():
        pl.semaphore_wait(ready.at[0], n_shard - 1)
        pl.semaphore_signal(ready.at[2], inc=1, device_id=(right, me_s), device_id_type=MESH)

    @pl.when(is_late | is_last)
    def _():
        pl.semaphore_wait(ready.at[2], 1)
        exchange()

    tiles_v[absent] = jnp.zeros((tile, tile), BF16)
    get_rows.wait()
    get_cols.wait()

    def block_matrix(j, cs):
        place = [rows_s[j, 0, t] * row_tiles + cols_s[j, 0, t] for t in range(tpb)]

        def pick_tile(r, c):
            at = jnp.int32(absent)
            for t in range(tpb):
                at = jnp.where(place[t] == r * row_tiles + c, j * tpb + t, at)
            return tiles_v[at]

        return jnp.concatenate(
            [
                jnp.concatenate([pick_tile(r, c) for c in cs], axis=1)
                for r in range(row_tiles)
            ],
            axis=0,
        )

    def times(j, cs, ref):
        x = ref[pl.ds(cs[0] * tile, len(cs) * tile), :]
        return jnp.dot(block_matrix(j, cs), x, preferred_element_type=F32)

    for copy in get_tiles.values():
        copy.wait()
    acc[...] = times(span, range(row_tiles), own)

    get_weight.wait()
    get_target.wait()
    get_value.wait()
    get_count.wait()
    spread_l = mask_of(iota((peers, lanes), 1) // slots == iota((peers, lanes), 0), BF16)
    slot_l = iota((slots, lanes), 1) % slots
    own_slot = slot_l == iota((slots, lanes), 0)

    def along(x):
        wide_x = jnp.dot(x, spread_l, preferred_element_type=F32)
        return jnp.sum(jnp.where(own_slot, wide_x, 0.0), axis=0, keepdims=True)

    target_l = along((target_v[...] - half).astype(F32).astype(BF16))
    value_l = along(value_v[...])
    count_l = jnp.dot(count_v[...].astype(F32).astype(BF16), spread_l, preferred_element_type=F32)
    live = (iota((1, lanes), 1) % slots).astype(F32) < count_l
    value_l = jnp.where(live, value_l, 0.0)
    placing = jnp.where(
        (iota((rows_dev, lanes), 0) - half).astype(F32) == target_l, value_l, 0.0
    ).astype(BF16)

    received[pl.ds(me_s * slots, slots), :] = outgoing[pl.ds(me_s * slots, slots), :]
    acc[...] += times(span - 1, every, arrived.at[0])
    acc[...] += times(span + 1, every, arrived.at[1])

    some = pl.ds(0, (n_shard - 1) * slots)
    pltpu.make_async_copy(received.at[some], received.at[some], sh_recv).wait()
    acc[...] += jnp.dot(placing, received[...], preferred_element_type=F32)
    for c in every:
        second[1, c].wait_recv()
    acc[...] += times(span + 2, every, arrived.at[3])

    for c in every:
        if c == 0:
            pl.when(jnp.logical_not(is_second))(second[0, c].wait_recv)
        else:
            second[0, c].wait_recv()
        if c == row_tiles - 2:
            @pl.when(is_first)
            def _():
                pl.semaphore_wait(ready.at[1], n_shard - 1)
                pl.semaphore_signal(ready.at[2], inc=1, device_id=(left, me_s), device_id_type=MESH)
        acc[...] += times(span - 2, [c], arrived.at[2])

    total = acc[...].astype(BF16)
    product = jnp.dot(total, weight_v[...], preferred_element_type=F32)
    out[0] = jnp.maximum(product, 0.0).astype(BF16)

    for copy in list(first.values()) + [second[0, c] for c in every]:
        copy.wait_send()

    @pl.when(jnp.logical_not(is_first))
    def _():
        for c in every:
            second[1, c].wait_send()

    @pl.when(is_third)
    def _():
        for copy in third:
            copy.wait_send()

    pltpu.make_async_copy(outgoing.at[some], outgoing.at[some], sh_send).wait()


def layer(mesh, features, tiles, t_rows, t_cols, send_rows, target, value, count, weight):
    n_blk, n_shard = mesh.shape["blk"], mesh.shape["shard"]
    _, rows_dev, feat = features.shape
    _, _, reach, tpb, tile, _ = tiles.shape
    assert reach == 5 and rows_dev <= 512 and rows_dev % tile == 0
    _, _, peers, slots = send_rows.shape
    row_tiles = rows_dev // tile
    lanes = peers * slots
    dma = pltpu.SemaphoreType.DMA
    flops = 2 * feat * (reach * rows_dev * rows_dev + 2 * rows_dev * lanes + rows_dev * feat)
    return pl.pallas_call(
        functools.partial(kernel, n_blk, n_shard),
        out_shape=pltpu.VMEM((1, rows_dev, feat), BF16),
        in_specs=[pl.BlockSpec(memory_space=pl.ANY)] * 9,
        out_specs=pl.BlockSpec(memory_space=pltpu.VMEM),
        scratch_shapes=[
            pltpu.VMEM((rows_dev, feat), BF16),
            pltpu.VMEM((reach * tpb + 1, tile, tile), BF16),
            pltpu.SMEM((reach, 1, tpb), jnp.int32),
            pltpu.SMEM((reach, 1, tpb), jnp.int32),
            pltpu.VMEM((slots, peers), jnp.int32),
            pltpu.VMEM((slots, peers), jnp.int32),
            pltpu.VMEM((slots, peers), BF16),
            pltpu.VMEM((1, peers), jnp.int32),
            pltpu.VMEM((feat, feat), BF16),
            pltpu.VMEM((lanes, feat), BF16),
            pltpu.VMEM((lanes, feat), BF16),
            pltpu.VMEM((4, rows_dev, feat), BF16),
            pltpu.VMEM((rows_dev, feat), F32),
            dma((8,)),
            dma((reach,)),
            dma((5, row_tiles)),
            dma((4, row_tiles)),
            dma,
            dma,
            pltpu.SemaphoreType.REGULAR((5,)),
            pltpu.SemaphoreType.REGULAR,
        ],
        compiler_params=pltpu.CompilerParams(
            collective_id=0, has_side_effects=True, vmem_limit_bytes=60 * 1024 * 1024
        ),
        cost_estimate=pl.CostEstimate(flops=flops, bytes_accessed=4 << 20, transcendentals=0),
    )(
        features,
        tiles,
        t_rows.transpose(0, 2, 1, 3),
        t_cols.transpose(0, 2, 1, 3),
        send_rows.transpose(0, 1, 3, 2),
        target.transpose(0, 1, 3, 2),
        value.transpose(0, 1, 3, 2),
        count,
        weight,
    )


def solution(mesh):
    return jax.shard_map(
        functools.partial(layer, mesh),
        mesh=mesh,
        in_specs=(
            P("shard", "blk", None),
            P("shard", "blk", None, None, None, None),
            P("shard", "blk", None, None),
            P("shard", "blk", None, None),
            P("shard", "blk", None, None),
            P("shard", "blk", None, None),
            P("shard", "blk", None, None),
            P("shard", "blk", None),
            P(),
        ),
        out_specs=P("shard", "blk", None),
        check_vma=False,
    )
```

```python
import functools

import jax
import jax.numpy as jnp
from jax import lax
from jax.experimental import pallas as pl
from jax.experimental.pallas import tpu as pltpu
from jax.sharding import PartitionSpec as P

MESH = pl.DeviceIdType.MESH
F32 = jnp.float32
BF16 = jnp.bfloat16


def iota(shape, axis):
    return lax.broadcasted_iota(jnp.int32, shape, axis)


def mask_of(cond, dtype):
    return jnp.where(cond, F32(1.0), F32(0.0)).astype(dtype)


def kernel(
    n_blk,
    n_shard,
    feats,
    tiles,
    t_rows,
    t_cols,
    send_rows,
    target,
    value,
    count,
    weight,
    out,
    own,
    tiles_v,
    rows_s,
    cols_s,
    send_v,
    target_v,
    value_v,
    count_v,
    weight_v,
    outgoing,
    received,
    arrived,
    acc,
    in_sem,
    tile_sem,
    blk_send,
    blk_recv,
    sh_send,
    sh_recv,
    ready,
    hello,
):
    rows_dev, feat = own.shape
    reach = tiles.shape[2]
    tpb = tiles.shape[3]
    tile = tiles.shape[4]
    span = (reach - 1) // 2
    row_tiles = rows_dev // tile
    slots, peers = send_v.shape
    lanes = peers * slots
    absent = reach * tpb
    me_b = lax.axis_index("blk")
    me_s = lax.axis_index("shard")
    right = lax.rem(me_b + 1, n_blk)
    left = lax.rem(me_b + n_blk - 1, n_blk)

    run = n_blk // 2
    left3 = lax.rem(me_b + n_blk - 3, n_blk)
    z = lax.rem(me_b, run)
    is_first, is_second, is_third, is_last, is_late = z == 0, z == 1, z == 2, z == run - 1, z == run - 2
    direct = z < run - 2
    before_late = z == run - 3
    def signal(sem, shard):
        pl.semaphore_signal(sem, inc=1, device_id=(me_b, shard), device_id_type=MESH)

    barrier = pltpu.get_barrier_semaphore()
    pl.semaphore_signal(barrier, inc=1, device_id=(left, me_s), device_id_type=MESH)

    def tell_all(sem):
        def tell(k, c):
            signal(sem, lax.rem(me_s + k, n_shard))
            return c

        lax.fori_loop(1, n_shard, tell, 0)

    straggler = (me_b == 0) & (me_s == 0)
    without = (me_b == 0) & (me_s != 0)
    pl.when(direct & jnp.logical_not(straggler))(lambda: tell_all(barrier))
    needed = jnp.where(without, n_shard - 1, n_shard)
    pl.semaphore_wait(barrier, jnp.where(direct, needed, 1))
    pl.when(straggler)(lambda: tell_all(ready.at[3]))

    pl.when(before_late)(lambda: tell_all(ready.at[0]))

    def piece(ref, c):
        return ref.at[pl.ds(c * tile, tile)]

    def pieces(src, dst, way, sent, c, to):
        return pltpu.make_async_remote_copy(
            src_ref=piece(src, c),
            dst_ref=piece(dst, c),
            send_sem=blk_send.at[sent, c],
            recv_sem=blk_recv.at[way, c],
            device_id=(to, me_s),
            device_id_type=MESH,
        )

    def send(src, dst, way, c, to):
        copy = pieces(src, dst, way, way, c, to)
        copy.start()
        return copy

    first = {}
    second = {}
    for c in range(row_tiles):
        first[0, c] = send(feats.at[0], arrived.at[0], 0, c, right)
        if c == 0:
            pl.semaphore_signal(hello, inc=1, device_id=(right, me_s), device_id_type=MESH)

    def local(src, dst, sem):
        copy = pltpu.make_async_copy(src, dst, sem)
        copy.start()
        return copy

    get_own = local(feats.at[0], own, in_sem.at[0])
    get_send = local(send_rows.at[0, 0], send_v, in_sem.at[1])
    get_rows = local(t_rows.at[0], rows_s, in_sem.at[2])
    get_cols = local(t_cols.at[0], cols_s, in_sem.at[3])
    get_tiles = {
        j: local(tiles.at[0, 0, j], tiles_v.at[pl.ds(j * tpb, tpb)], tile_sem.at[j])
        for j in range(reach)
    }
    get_target = local(target.at[0, 0], target_v, in_sem.at[4])
    get_value = local(value.at[0, 0], value_v, in_sem.at[5])
    get_count = local(count.at[0], count_v, in_sem.at[6])
    get_weight = local(weight, weight_v, in_sem.at[7])

    half = rows_dev // 2

    def gather():
        spread = mask_of(iota((lanes, peers), 0) // slots == iota((lanes, peers), 1), BF16)
        picks = (send_v[...] - half).astype(F32).astype(BF16)
        mine = lax.dot_general(spread, picks, (((1,), (1,)), ((), ())), preferred_element_type=F32)
        mine = jnp.where(iota((lanes, slots), 0) % slots == iota((lanes, slots), 1), mine, 0.0)
        wide = jnp.dot(mine.astype(BF16), jnp.ones((slots, 128), BF16), preferred_element_type=F32)
        pick = jnp.concatenate(
            [
                mask_of(wide == (iota((lanes, 128), 1) + (g * 128 - half)).astype(F32), BF16)
                for g in range(rows_dev // 128)
            ],
            axis=1,
        )
        outgoing[...] = jnp.dot(pick, own[...], preferred_element_type=F32).astype(BF16)

    def give(k):
        to = lax.rem(me_s + k, n_shard)
        pltpu.make_async_remote_copy(
            src_ref=outgoing.at[pl.ds(to * slots, slots)],
            dst_ref=received.at[pl.ds(me_s * slots, slots)],
            send_sem=sh_send,
            recv_sem=sh_recv,
            device_id=(me_b, to),
            device_id_type=MESH,
        ).start()

    def exchange():
        gather()
        far = n_shard // 2

        def but(k):
            skip = without & (lax.rem(me_s + k, n_shard) == 0)
            pl.when(jnp.logical_not(skip))(lambda: give(k))

        but(far)

        def both(i, c):
            but(far - i)
            but(far + i)
            return c

        lax.fori_loop(1, far, both, 0)

    get_send.wait()
    get_own.wait()
    pl.when(direct)(exchange)

    @pl.when(without)
    def _():
        pl.semaphore_wait(ready.at[3], 1)
        give(n_shard - me_s)

    pl.semaphore_wait(hello, 1)

    pl.when(is_first)(lambda: tell_all(ready.at[1]))

    for c in range(row_tiles):
        first[1, c] = send(feats.at[0], arrived.at[1], 1, c, left)

    every = range(row_tiles)
    for c in every:
        first[0, c].wait_recv()
        second[0, c] = send(arrived.at[0], arrived.at[2], 2, c, right)
    for c in every:
        first[1, c].wait_recv()
        second[1, c] = pieces(arrived.at[1], arrived.at[3], 3, 3, c, left)
        pl.when(jnp.logical_not(is_first))(second[1, c].start)

    third = [pieces(arrived.at[0], arrived.at[3], 3, 4, c, left3) for c in every]

    @pl.when(is_second)
    def _():
        second[0, 0].wait_recv()
        pl.semaphore_signal(ready.at[4], inc=1, device_id=(right, me_s), device_id_type=MESH)

    @pl.when(is_third)
    def _():
        pl.semaphore_wait(ready.at[4], 1)
        for copy in third:
            copy.start()

    @pl.when(before_late)
    def _():
        pl.semaphore_wait(ready.at[0], n_shard - 1)
        pl.semaphore_signal(ready.at[2], inc=1, device_id=(right, me_s), device_id_type=MESH)

    @pl.when(is_late | is_last)
    def _():
        pl.semaphore_wait(ready.at[2], 1)
        exchange()

    tiles_v[absent] = jnp.zeros((tile, tile), BF16)
    get_rows.wait()
    get_cols.wait()

    def block_matrix(j, cs):
        place = [rows_s[j, 0, t] * row_tiles + cols_s[j, 0, t] for t in range(tpb)]

        def pick_tile(r, c):
            at = jnp.int32(absent)
            for t in range(tpb):
                at = jnp.where(place[t] == r * row_tiles + c, j * tpb + t, at)
            return tiles_v[at]

        return jnp.concatenate(
            [
                jnp.concatenate([pick_tile(r, c) for c in cs], axis=1)
                for r in range(row_tiles)
            ],
            axis=0,
        )

    def times(j, cs, ref):
        x = ref[pl.ds(cs[0] * tile, len(cs) * tile), :]
        return jnp.dot(block_matrix(j, cs), x, preferred_element_type=F32)

    for copy in get_tiles.values():
        copy.wait()
    acc[...] = times(span, range(row_tiles), own)

    get_weight.wait()
    get_target.wait()
    get_value.wait()
    get_count.wait()
    spread_l = mask_of(iota((peers, lanes), 1) // slots == iota((peers, lanes), 0), BF16)
    slot_l = iota((slots, lanes), 1) % slots
    own_slot = slot_l == iota((slots, lanes), 0)

    def along(x):
        wide_x = jnp.dot(x, spread_l, preferred_element_type=F32)
        return jnp.sum(jnp.where(own_slot, wide_x, 0.0), axis=0, keepdims=True)

    target_l = along((target_v[...] - half).astype(F32).astype(BF16))
    value_l = along(value_v[...])
    count_l = jnp.dot(count_v[...].astype(F32).astype(BF16), spread_l, preferred_element_type=F32)
    live = (iota((1, lanes), 1) % slots).astype(F32) < count_l
    value_l = jnp.where(live, value_l, 0.0)
    placing = jnp.where(
        (iota((rows_dev, lanes), 0) - half).astype(F32) == target_l, value_l, 0.0
    ).astype(BF16)

    received[pl.ds(me_s * slots, slots), :] = outgoing[pl.ds(me_s * slots, slots), :]
    acc[...] += times(span - 1, every, arrived.at[0])
    acc[...] += times(span + 1, every, arrived.at[1])

    some = pl.ds(0, (n_shard - 1) * slots)
    pltpu.make_async_copy(received.at[some], received.at[some], sh_recv).wait()
    acc[...] += jnp.dot(placing, received[...], preferred_element_type=F32)
    for c in every:
        second[1, c].wait_recv()
    acc[...] += times(span + 2, every, arrived.at[3])

    for c in every:
        if c == 0:
            pl.when(jnp.logical_not(is_second))(second[0, c].wait_recv)
        else:
            second[0, c].wait_recv()
        if c == row_tiles - 2:
            @pl.when(is_first)
            def _():
                pl.semaphore_wait(ready.at[1], n_shard - 1)
                pl.semaphore_signal(ready.at[2], inc=1, device_id=(left, me_s), device_id_type=MESH)
        acc[...] += times(span - 2, [c], arrived.at[2])

    total = acc[...].astype(BF16)
    product = jnp.dot(total, weight_v[...], preferred_element_type=F32)
    out[0] = jnp.maximum(product, 0.0).astype(BF16)

    for copy in list(first.values()) + [second[0, c] for c in every]:
        copy.wait_send()

    @pl.when(jnp.logical_not(is_first))
    def _():
        for c in every:
            second[1, c].wait_send()

    @pl.when(is_third)
    def _():
        for copy in third:
            copy.wait_send()

    pltpu.make_async_copy(outgoing.at[some], outgoing.at[some], sh_send).wait()


def layer(mesh, features, tiles, t_rows, t_cols, send_rows, target, value, count, weight):
    n_blk, n_shard = mesh.shape["blk"], mesh.shape["shard"]
    _, rows_dev, feat = features.shape
    _, _, reach, tpb, tile, _ = tiles.shape
    assert reach == 5 and rows_dev <= 512 and rows_dev % tile == 0
    _, _, peers, slots = send_rows.shape
    row_tiles = rows_dev // tile
    lanes = peers * slots
    dma = pltpu.SemaphoreType.DMA
    flops = 2 * feat * (reach * rows_dev * rows_dev + 2 * rows_dev * lanes + rows_dev * feat)
    return pl.pallas_call(
        functools.partial(kernel, n_blk, n_shard),
        out_shape=pltpu.VMEM((1, rows_dev, feat), BF16),
        in_specs=[pl.BlockSpec(memory_space=pl.ANY)] * 9,
        out_specs=pl.BlockSpec(memory_space=pltpu.VMEM),
        scratch_shapes=[
            pltpu.VMEM((rows_dev, feat), BF16),
            pltpu.VMEM((reach * tpb + 1, tile, tile), BF16),
            pltpu.SMEM((reach, 1, tpb), jnp.int32),
            pltpu.SMEM((reach, 1, tpb), jnp.int32),
            pltpu.VMEM((slots, peers), jnp.int32),
            pltpu.VMEM((slots, peers), jnp.int32),
            pltpu.VMEM((slots, peers), BF16),
            pltpu.VMEM((1, peers), jnp.int32),
            pltpu.VMEM((feat, feat), BF16),
            pltpu.VMEM((lanes, feat), BF16),
            pltpu.VMEM((lanes, feat), BF16),
            pltpu.VMEM((4, rows_dev, feat), BF16),
            pltpu.VMEM((rows_dev, feat), F32),
            dma((8,)),
            dma((reach,)),
            dma((5, row_tiles)),
            dma((4, row_tiles)),
            dma,
            dma,
            pltpu.SemaphoreType.REGULAR((5,)),
            pltpu.SemaphoreType.REGULAR,
        ],
        compiler_params=pltpu.CompilerParams(
            collective_id=0, has_side_effects=True, vmem_limit_bytes=60 * 1024 * 1024
        ),
        cost_estimate=pl.CostEstimate(flops=flops, bytes_accessed=4 << 20, transcendentals=0),
    )(
        features,
        tiles,
        t_rows.transpose(0, 2, 1, 3),
        t_cols.transpose(0, 2, 1, 3),
        send_rows.transpose(0, 1, 3, 2),
        target.transpose(0, 1, 3, 2),
        value.transpose(0, 1, 3, 2),
        count,
        weight,
    )


def solution(mesh):
    return jax.shard_map(
        functools.partial(layer, mesh),
        mesh=mesh,
        in_specs=(
            P("shard", "blk", None),
            P("shard", "blk", None, None, None, None),
            P("shard", "blk", None, None),
            P("shard", "blk", None, None),
            P("shard", "blk", None, None),
            P("shard", "blk", None, None),
            P("shard", "blk", None, None),
            P("shard", "blk", None),
            P(),
        ),
        out_specs=P("shard", "blk", None),
        check_vma=False,
    )
```
